512 devices in a mesh: pulse: 64 (over z, x), range: 8 (over y, core).
Axes of the slice: x: 4, y: 4, z: 16, core: 2. Of those that a mesh axis runs over, the one named last changes fastest.
Arguments:
- echo: bfloat16 [128, 2, 32768], P('pulse', None, 'range'), may hold values from -6 to 6
- chirp_phase: float32 [256], replicated, may hold values from -0.5 to 201.5624
- rec_phase: float32 [8, 8192, 2], P('range', 'pulse'), may hold values from -3.140625 to 3.140625
- rec_start: int32 [8, 8192], P('range', 'pulse'), may hold values from 0 to 32256
- rec_owner: int32 [8, 8192, 1], P('range', 'pulse'), may hold values from 0 to 511; in each aligned block of 128 rows (0 to 127, 128 to 255, ..., all dimensions but the last counted through in order) at most 2 rows name the same one
- rec_row: int32 [8, 8192], P('range', 'pulse'), may hold values from 0 to 63
- rec_weight: float32 [8, 8192], P('range', 'pulse'), may hold values from 0.2 to 1
- rec_count: int32 [8, 64], P('range', 'pulse'), may hold values from 96 to 128, as said below
- prior: bfloat16 [2048, 2, 4096], P('pulse', None, 'range'), may hold values from -6 to 6
- interp_weight: bfloat16 [64, 32], replicated, may hold values from -1 to 1
Outputs:
- tiles: float32 [4096, 2, 4096], P('pulse', None, 'range')
The draws below stay inside these ranges and needn't reach their ends.
Inputs may be any that keep to these rules, and one draw needn't show every extreme that they name: `rec_owner`: in each aligned block of 128 record slots (one device's slots) no owner is named more than 2 times. Owner o is the tile of pulse index o // 8 and range index o % 8, 8 being the number of range devices. `rec_count`: some subimage has all 128 slots live.
All inputs are finite; a program needn't handle non-finite values.
Results may differ from the reference program's by a relative error of at most 0.0034.
Values may be sent and summed in bfloat16 or wider, within the bound.
A program may use at most 64 MiB of HBM per device.

```python
import math
import jax
import jax.numpy as jnp
import numpy as np
from jax import lax

RANGE = 32768
TAPS = 256
SEG = 512
PD = 2
REC = 128
OUT_ROWS = 64
PRIOR = 32
PULSES = 128
RECS = 8192
CAP = 2
N_PULSE = 64
N_RANGE = 8
DEVICES = 512


def draw_chirp_phase(key, part):
    rate_key, noise_key = jax.random.split(key)
    sweep_rate = jax.random.uniform(rate_key, (), jnp.float32, 0.6, 1.0)
    offset = jnp.arange(TAPS, dtype=jnp.float32) - TAPS / 2
    jitter = jax.random.uniform(noise_key, (TAPS,), jnp.float32, -0.5, 0.5)
    return math.pi * sweep_rate * offset * offset / TAPS + jitter


def draw_rec_count(key, part):
    count_key, row_key, col_key = jax.random.split(key, 3)
    counts = jax.random.randint(count_key, (N_RANGE, N_PULSE), 3 * REC // 4, REC + 1)
    row_pick = jax.random.randint(row_key, (), 0, N_RANGE)
    col_pick = jax.random.randint(col_key, (), 0, N_PULSE)
    return counts.at[row_pick, col_pick].set(REC)


def set_ends(array, key, least, largest):
    extent = array.shape
    spot = [jax.random.randint(jax.random.fold_in(key, axis), (), 0, extent[axis]) for axis in range(len(extent))]
    array = array.at[tuple(spot)].set(least)
    longest = extent.index(max(extent))
    spot[longest] = (spot[longest] + 1) % extent[longest]
    return array.at[tuple(spot)].set(largest)


def levels(key, shape, cuts, low, high):
    loudness, own = 1.0, jax.random.fold_in(key, 6)
    for position, parts in cuts:
        draws = jnp.exp(jax.random.uniform(jax.random.fold_in(own, position), (parts,), jnp.float32, low / len(cuts), high / len(cuts)))
        loudness = loudness * jnp.repeat(draws, shape[position] // parts).reshape([-1 if axis == position else 1 for axis in range(len(shape))])
    return loudness


def deal_out(own_key, own, number, rows, count, top, bound, lean):
    order = jax.random.permutation(own_key, count)
    packed, common = portions_of(count, rows * top, bound, lean, True), portions_of(count, rows * top, bound, lean, False)
    places = jnp.arange(count)

    def named(sizes, turn):
        used = int((sizes > 0).sum())
        fixed = max(1, used // 4)
        shifted = fixed + (places - fixed + turn * (used - fixed)) % max(1, count - fixed)
        return jnp.zeros((count,), jnp.int32).at[order[jnp.where(places < fixed, places, shifted)]].set(jnp.asarray(sizes, jnp.int32))

    sizes = jnp.where(number % 4 == 0, named(packed, number // 4), named(common, number - number // 4 - 1))
    mixed = jax.random.permutation(jax.random.fold_in(own, 3), count)
    source_of, taker = mixed[0:count // 2 * 2:2], mixed[1:count // 2 * 2:2]
    room = jnp.minimum(sizes[source_of] - 1, bound - sizes[taker]) // 2
    room = jnp.where((source_of == order[0]) | (taker == order[0]) | (sizes[taker] == 0), 0, jnp.maximum(room, 0))
    shifted = jax.random.randint(jax.random.fold_in(own, 4), (count // 2,), 0, 1 << 20) % (room + 1)
    sizes = sizes.at[source_of].add(-shifted).at[taker].add(shifted)
    members = jnp.searchsorted(jnp.cumsum(sizes), jnp.arange(rows * top), side="right").astype(jnp.int32)
    grid = members.reshape(top, rows).T
    grid = grid[jax.random.permutation(jax.random.fold_in(own, 1), rows)]
    turn = jax.random.randint(jax.random.fold_in(own, 2), (rows, 1), 0, top)
    return jnp.take_along_axis(grid, (jnp.arange(top)[None, :] + turn) % top, axis=1)


def portions_of(count, total, bound, skew, full):
    portions = [(1 << 20) // math.isqrt(rank ** skew) + 1 for rank in range(1, count + 1)]
    largest = bound if full else min(bound, max(-(-total // count), total * portions[0] // sum(portions)))
    least = 1 if total - largest >= count - 1 else 0
    given, surplus = [largest] + [least] * (count - 1), total - largest - least * (count - 1)
    while surplus > 0:
        free = [i for i in range(1, count) if given[i] < largest] or [i for i in range(1, count) if given[i] < bound]
        pool, remaining = sum([portions[i] for i in free]), surplus
        for i in free:
            addition = min(bound - given[i], max(1, remaining * portions[i] // pool), surplus)
            given[i] = given[i] + addition
            surplus = surplus - addition
    return np.array(given)


def bell_draw(stream_key, dims, deviation, limit, shards=(), held_as=jnp.bfloat16):
    array = jax.random.normal(stream_key, dims, jnp.float32) * deviation
    if len(shards) > 0:
        array = levels(stream_key, dims, shards, -0.22, 0.18) * array
    return jnp.clip(array, min=-limit, max=limit).astype(held_as)


def setup_inputs(seed: int = 0) -> dict:
    seeds = jax.random.split(jax.random.key(seed), 11)
    echo = bell_draw(seeds[0], (PULSES, 2, RANGE), 1.0, 6.0, ((0, 64), (2, 8)))
    chirp_phase = draw_chirp_phase(jax.random.fold_in(seeds[10], 71), 0)
    rec_phase = jnp.clip(jax.random.uniform(seeds[2], (N_RANGE, RECS, PD), jnp.float32, -3.140625, 3.140625), -3.140625, 3.140625)
    rec_start = set_ends(jax.random.randint(seeds[3], (N_RANGE, RECS), 0, RANGE - SEG + 1), jax.random.fold_in(seeds[3], 1), 0, RANGE - SEG).astype(jnp.int32)
    rec_owner_keys = jax.random.split(jax.random.fold_in(seeds[4], 1), N_RANGE * RECS // REC)
    rec_owner_turns = jax.random.permutation(jax.random.fold_in(seeds[4], 3), N_RANGE * RECS // REC)
    rec_owner = jax.vmap(lambda own, number: deal_out(jax.random.fold_in(seeds[4], 2), own, number, REC, DEVICES, 1, CAP, 2))(rec_owner_keys, rec_owner_turns).reshape((N_RANGE, RECS, 1))
    rec_row = set_ends(jax.random.randint(seeds[5], (N_RANGE, RECS), 0, OUT_ROWS), jax.random.fold_in(seeds[5], 1), 0, OUT_ROWS - 1).astype(jnp.int32)
    rec_weight = jnp.clip(0.2 + 0.8 * jax.random.uniform(seeds[6], (N_RANGE, RECS), jnp.float32) ** levels(seeds[6], (N_RANGE, RECS), ((0, 8), (1, 64)), -0.2, 0.2), 0.2, 1.0)
    rec_count = draw_rec_count(jax.random.fold_in(seeds[10], 71), 0)
    prior = bell_draw(seeds[8], (N_PULSE * PRIOR, 2, N_RANGE * SEG), 1.0, 6.0, ((0, 64), (2, 8)))
    interp_weight = bell_draw(seeds[9], (OUT_ROWS, PRIOR), PRIOR ** -0.5, 1.0)
    return dict(echo=echo, chirp_phase=chirp_phase, rec_phase=rec_phase, rec_start=rec_start, rec_owner=rec_owner, rec_row=rec_row, rec_weight=rec_weight, rec_count=rec_count, prior=prior, interp_weight=interp_weight)


def chirp_matrix(chirp_phase):
    tap_count = chirp_phase.shape[0]
    tap_scale = 1.0 / jnp.sqrt(jnp.float32(tap_count))
    real_taps = jnp.cos(chirp_phase) * tap_scale
    imag_taps = jnp.sin(chirp_phase) * tap_scale

    def banded(values):
        padded = jnp.concatenate([values, jnp.zeros((tap_count + 1,), jnp.float32)])
        return jnp.tile(padded, tap_count)[:2 * tap_count * tap_count].reshape(tap_count, 2 * tap_count).T
    real_band = banded(real_taps)
    imag_band = banded(imag_taps)
    upper = jnp.concatenate([real_band, -imag_band], axis=1)
    lower = jnp.concatenate([imag_band, real_band], axis=1)
    return jnp.concatenate([upper, lower], axis=0).astype(jnp.bfloat16)

def compress(echo_block, tail_rim, filter_matrix):
    pulses, planes, bin_count = echo_block.shape
    tap_count = filter_matrix.shape[1] // 2
    block_count = bin_count // tap_count
    extended = jnp.concatenate([echo_block, tail_rim], axis=2)
    left_half = extended[:, :, :bin_count].reshape(pulses, planes, block_count, tap_count)
    right_half = extended[:, :, tap_count:].reshape(pulses, planes, block_count, tap_count)
    windows = jnp.concatenate([left_half, right_half], axis=3)
    windows = windows.transpose(0, 2, 1, 3).reshape(pulses * block_count, 2 * planes * tap_count)
    filtered = jnp.dot(windows, filter_matrix, preferred_element_type=jnp.float32)
    filtered = filtered.reshape(pulses, block_count, planes, tap_count).transpose(0, 2, 1, 3)
    return filtered.reshape(pulses, planes, bin_count).astype(jnp.bfloat16)

def form_records(profiles, starts, phases, scales):

    def window_at(start):
        return lax.dynamic_slice_in_dim(profiles, start, SEG, 2)
    windows = jax.vmap(window_at)(starts).astype(jnp.float32)
    cosine = jnp.cos(phases).astype(jnp.bfloat16).astype(jnp.float32)
    sine_part = jnp.sin(phases).astype(jnp.bfloat16).astype(jnp.float32)
    real_part = windows[:, :, 0]
    imag_part = windows[:, :, 1]
    out_real = jnp.einsum('bk,bks->bs', cosine, real_part) - jnp.einsum('bk,bks->bs', sine_part, imag_part)
    out_imag = jnp.einsum('bk,bks->bs', cosine, imag_part) + jnp.einsum('bk,bks->bs', sine_part, real_part)
    return jnp.stack([out_real, out_imag], axis=1) * scales[:, None, None]

def reference(echo, chirp_phase, rec_phase, rec_start, rec_owner, rec_row, rec_weight, rec_count, prior, interp_weight):
    filter_matrix = chirp_matrix(chirp_phase)
    grouped = echo.reshape(N_PULSE, PD, 2, RANGE)
    empty_rim = jnp.zeros((PD, 2, TAPS), echo.dtype)
    compressed = lax.map(lambda group: compress(group, empty_rim, filter_matrix), grouped)

    def by_pulse(values):
        shaped = values.reshape((N_RANGE, N_PULSE, REC) + values.shape[2:])
        order = (1, 0, 2) + tuple(range(3, shaped.ndim))
        return shaped.transpose(order).reshape((N_PULSE, N_RANGE * REC) + values.shape[2:])
    starts = by_pulse(rec_start).astype(jnp.int32)
    phases = by_pulse(rec_phase)
    owners = by_pulse(rec_owner[:, :, 0]).astype(jnp.int32)
    dest_rows = by_pulse(rec_row).astype(jnp.int32)
    live_mask = (jnp.arange(REC)[None, None, :] < rec_count[:, :, None]).astype(jnp.float32)
    scales = live_mask * rec_weight.reshape(N_RANGE, N_PULSE, REC) / jnp.sqrt(jnp.float32(PD))
    scales = scales.transpose(1, 0, 2).reshape(N_PULSE, N_RANGE * REC)
    targets = ((owners // N_RANGE * OUT_ROWS + dest_rows) * N_RANGE + owners % N_RANGE).astype(jnp.int32)
    initial = jnp.zeros((N_PULSE * OUT_ROWS * N_RANGE, 2, SEG), jnp.float32)

    def add_subimage(total, items):
        profiles, start_list, phase_list, scale_list, target_list = items
        records = form_records(profiles, start_list, phase_list, scale_list)
        rounded = lax.optimization_barrier(records.astype(jnp.bfloat16))
        return (total.at[target_list].add(rounded.astype(jnp.float32)), None)
    total, _ = lax.scan(add_subimage, initial, (compressed, starts, phases, scales, targets))
    total = total.reshape(N_PULSE * OUT_ROWS, N_RANGE, 2, SEG).transpose(0, 2, 1, 3)
    total = total.reshape(N_PULSE * OUT_ROWS, 2, N_RANGE * SEG)
    coarse = prior.astype(jnp.float32).reshape(N_PULSE, PRIOR, 2 * N_RANGE * SEG)
    fine = jnp.einsum('rm,qmx->qrx', interp_weight.astype(jnp.float32), coarse, precision=lax.Precision.HIGHEST)
    fine = fine.reshape(N_PULSE * OUT_ROWS, 2, N_RANGE * SEG)
    return fine + total
```

```python
import functools

import jax
import jax.numpy as jnp
from jax import lax
from jax.experimental import pallas as pl
from jax.experimental.pallas import tpu as pltpu
from jax.sharding import PartitionSpec as P

MESH = pl.DeviceIdType.MESH
LANES = 128
NT = (((1,), (1,)), ((), ()))


def position():
    pulse, rng = lax.axis_index("pulse"), lax.axis_index("range")
    return pulse // 4, lax.rem(pulse, 4), rng // 2, lax.rem(rng, 2)


def at(z, x, y, c):
    return (lax.rem(z + 16, 16) * 4 + lax.rem(x + 4, 4), lax.rem(y + 4, 4) * 2 + c)


def swap_planes(rows):
    count = rows.shape[0]
    even = lax.rem(lax.broadcasted_iota(jnp.int32, rows.shape, 0), 2) == 0
    return jnp.where(even, pltpu.roll(rows, count - 1, 0), -pltpu.roll(rows, 1, 0))


def gather_kernel(
    echo_ref, tap_cos_ref, tap_sin_ref, cos_ref, sin_ref, start_ref, owner_ref, owner_col_ref,
    row_ref, weight_ref, count_ref,
    prof_ref, meta_ref,
    ext, halo, own, own_meta, local_sem,
    halo_s, halo_r, z_s, z_r, mz_s, mz_r, a_s, a_r, b_s, b_r, t_s, t_r,
):
    z, x, y, c = position()
    twin = at(z, x, y, 1 - c)
    rng = y * 2 + c
    before = (lax.axis_index("pulse"), lax.rem(rng + 7, 8))
    after = (lax.axis_index("pulse"), lax.rem(rng + 1, 8))
    barrier = pltpu.get_barrier_semaphore()
    partners = [twin, before, after]
    for d in (1, 2, 3):
        partners += [at(z + 4 * d, x, y, c), at(z, x + d, y, c), at(z, x, y + d, c)]
    for partner in partners:
        pl.semaphore_signal(barrier, inc=1, device_id=partner, device_id_type=MESH)

    lanes = lax.broadcasted_iota(jnp.int32, (1, LANES), 1)
    sub = lax.broadcasted_iota(jnp.int32, (LANES, LANES), 0)
    lane2 = lax.broadcasted_iota(jnp.int32, (LANES, LANES), 1)
    earlier = (owner_col_ref[...] == owner_ref[...]) & (sub < lane2)
    rank = jnp.sum(earlier.astype(jnp.float32), axis=0, keepdims=True)
    live = lanes < count_ref[...]
    key = jnp.where(live, owner_ref[...].astype(jnp.float32) * 2.0 + rank, -1.0)
    scale = jnp.where(live, weight_ref[...], 0.0) * jnp.float32(0.5**0.5)
    fields = [key, start_ref[...].astype(jnp.float32), row_ref[...].astype(jnp.float32)]
    for k in range(2):
        fields += [scale * cos_ref[k : k + 1, :], scale * sin_ref[k : k + 1, :]]
    which = lax.broadcasted_iota(jnp.int32, (8, LANES), 0)
    tile = jnp.zeros((8, LANES), jnp.float32)
    for number, field in enumerate(fields):
        tile = jnp.where(which == number, field, tile)
    own_meta[...] = tile

    for k in range(2):
        ext[k, 0:64, :] = echo_ref[k * 64 : k * 64 + 64, :].astype(jnp.float32)
        halo[0, k * 4 : k * 4 + 4, :] = ext[k, 0:4, :]
    bands = []
    for ref in (tap_cos_ref, tap_sin_ref):
        taps = jnp.concatenate([ref[...], jnp.zeros((1, LANES), jnp.float32)], axis=1)
        taps = jnp.broadcast_to(taps, (LANES, 3 * LANES))
        bands.append(pltpu.roll(taps, 0, 1, stride=1, stride_axis=0).astype(jnp.bfloat16))
    band = jnp.concatenate(bands, axis=1)

    pl.semaphore_wait(barrier, len(partners))

    sends = []

    def send(src, dst, s, r, to):
        copy = pltpu.make_async_remote_copy(
            src_ref=src, dst_ref=dst, send_sem=s, recv_sem=r, device_id=to, device_id_type=MESH
        )
        copy.start()
        sends.append(copy)
        return copy

    halo_copy = send(halo.at[0], halo.at[1], halo_s, halo_r, before)
    mz = [
        send(own_meta, meta_ref.at[4 - d, x, y, c], mz_s.at[d - 1], mz_r.at[d - 1], at(z + 4 * d, x, y, c))
        for d in (1, 2, 3)
    ]
    keep_meta = pltpu.make_async_copy(own_meta, meta_ref.at[0, x, y, c], local_sem.at[0])
    keep_meta.start()
    halo_copy.wait_recv()
    inside = (rng < 7).astype(jnp.float32)
    for k in range(2):
        ext[k, 64:68, :] = halo[1, k * 4 : k * 4 + 4, :] * inside
        ext[k, 68:72, :] = jnp.zeros((4, LANES), jnp.float32)
    for k in range(2):
        whole = ext[k]
        swapped = swap_planes(whole)
        parts = [whole[2 * d : 2 * d + 64] for d in range(3)] + [swapped[2 * d : 2 * d + 64] for d in range(3)]
        windows = jnp.concatenate([part.astype(jnp.bfloat16) for part in parts], axis=1)
        filtered = lax.dot_general(windows, band, NT, preferred_element_type=jnp.float32)
        own[k] = filtered.astype(jnp.bfloat16)
    zs = [
        send(own, prof_ref.at[:, 4 - d, x, y, c], z_s.at[d - 1], z_r.at[d - 1], at(z + 4 * d, x, y, c))
        for d in (1, 2, 3)
    ]
    keep = pltpu.make_async_copy(own, prof_ref.at[:, 0, x, y, c], local_sem.at[1])
    keep.start()
    keep.wait()
    keep_meta.wait()

    near, far = pl.ds(0, 1), pl.ds(1, 3)


    def x_first(n, cut, zcut):
        first = [
            send(cut(zcut, x, y), cut(zcut, x, y), a_s.at[n, d - 1], a_r.at[n, d - 1], at(z, x + d, y, c))
            for d in (1, 2, 3)
        ]
        return n, cut, zcut, first, True

    def y_first(n, cut, zcut):
        first = [
            send(cut(zcut, x, y), cut(zcut, x, y), a_s.at[n, d - 1], a_r.at[n, d - 1], at(z, x, y + d, c))
            for d in (1, 2, 3)
        ]
        return n, cut, zcut, first, False

    def second(state):
        n, cut, zcut, first, xfirst = state
        for copy in first:
            copy.wait_recv()
        line = cut(zcut, slice(None), y) if xfirst else cut(zcut, x, slice(None))
        again = [
            send(
                line, line, b_s.at[n, d - 1], b_r.at[n, d - 1],
                at(z, x, y + d, c) if xfirst else at(z, x + d, y, c),
            )
            for d in (1, 2, 3)
        ]
        over = [send(line, line, t_s.at[n, 0], t_r.at[n, 0], twin)]
        return n, cut, zcut, again, over, xfirst

    def third(state):
        n, cut, zcut, again, over, xfirst = state
        for d, copy in zip((1, 2, 3), again):
            copy.wait_recv()
            line = (
                cut(zcut, slice(None), lax.rem(y + 4 - d, 4)) if xfirst else cut(zcut, lax.rem(x + 4 - d, 4), slice(None))
            )
            over.append(send(line, line, t_s.at[n, d], t_r.at[n, d], twin))
        return over

    def cut_of(k):
        return lambda zcut, x_, y_: prof_ref.at[k, zcut, x_, y_, c]

    def cut_meta(zcut, x_, y_):
        return meta_ref.at[zcut, x_, y_, c]

    first0 = x_first(0, cut_of(0), near)
    first1 = y_first(1, cut_of(1), near)
    for copy in mz:
        copy.wait_recv()
    first_m = x_first(4, cut_meta, pl.ds(0, 4))
    second0 = second(first0)
    second1 = second(first1)
    for copy in zs:
        copy.wait_recv()
    first2 = x_first(2, cut_of(0), far)
    first3 = y_first(3, cut_of(1), far)
    second_m = second(first_m)
    overs = third(second0) + third(second1)
    second2 = second(first2)
    second3 = second(first3)
    overs += third(second_m)
    overs += third(second2) + third(second3)
    for copy in overs:
        copy.wait_recv()
    for copy in sends:
        copy.wait_send()


def gather(echo_rows, tap_cos, tap_sin, cos, sin, start, owner, owner_col, row, weight, count):
    vmem = pl.BlockSpec(memory_space=pltpu.VMEM)
    dma = pltpu.SemaphoreType.DMA
    return pl.pallas_call(
        gather_kernel,
        out_shape=(
            jax.ShapeDtypeStruct((2, 4, 4, 4, 2, 64, LANES), jnp.bfloat16),
            jax.ShapeDtypeStruct((4, 4, 4, 2, 8, LANES), jnp.float32),
        ),
        in_specs=[vmem] * 11,
        out_specs=(pl.BlockSpec(memory_space=pl.ANY),) * 2,
        scratch_shapes=[
            pltpu.VMEM((2, 72, LANES), jnp.float32),
            pltpu.VMEM((2, 8, LANES), jnp.float32),
            pltpu.VMEM((2, 64, LANES), jnp.bfloat16),
            pltpu.VMEM((8, LANES), jnp.float32),
            dma((2,)),
            dma, dma, dma((3,)), dma((3,)), dma((3,)), dma((3,)),
            dma((5, 3)), dma((5, 3)), dma((5, 3)), dma((5, 3)), dma((5, 4)), dma((5, 4)),
        ],
        compiler_params=pltpu.CompilerParams(collective_id=0, has_side_effects=True, vmem_limit_bytes=16 << 20),
        name="gather",
    )(echo_rows, tap_cos, tap_sin, cos, sin, start, owner, owner_col, row, weight, count)


ROWS = 512


def merge_kernel(
    prof_in, meta_in, prior_ref, interp_ref, part_ref, base_ref, prof, acc, sel_i, sel_f, smem_i, smem_f, sems
):
    z, x, y, c = position()
    rng = y * 2 + c
    lanes = lax.broadcasted_iota(jnp.int32, (8, LANES), 1)
    sub = lax.broadcasted_iota(jnp.int32, (8, LANES), 0)

    keys = []
    for k in range(8):
        zo = lax.rem(z + (k // 2) + 15 - c, 16)
        keys.append(((((zo * 4 + x) * 8) + rng) * 2 + k % 2).astype(jnp.float32))

    @pl.loop(0, 8)
    def _(g):
        picked = jnp.zeros((8, LANES), jnp.float32)
        for t in range(16):
            tile = meta_in[g * 16 + t]
            key = tile[0:1, :]
            for k in range(8):
                one = jnp.sum(jnp.where(key == keys[k], tile, 0.0), axis=1, keepdims=True)
                picked = jnp.where(lanes == t * 8 + k, one, picked)
        whole = picked.astype(jnp.int32)
        start, row = whole[1:2, :], whole[2:3, :]
        lane = lanes[0:1, :]
        place = (g * 2 + lane // 64) * (2 * ROWS) + 2 * (start // LANES)
        target = lax.rem(lane, 8) // 2 * 64 + row
        ints = jnp.where(sub == 0, place, jnp.where(sub == 1, lax.rem(start, LANES), target))
        sel_i[g] = ints
        sel_f[g] = picked

    copies = [
        pltpu.make_async_copy(sel_i, smem_i, sems.at[0]),
        pltpu.make_async_copy(sel_f, smem_f, sems.at[1]),
    ]
    for copy in copies:
        copy.start()

    for k in range(2):

        @pl.loop(0, 16)
        def _(p):
            at_row = pl.multiple_of(p * (2 * ROWS) + k * ROWS, ROWS)
            prof[pl.ds(at_row, ROWS), :] = prof_in[k, p].astype(jnp.float32)

    prof[32 * ROWS : 32 * ROWS + 16, :] = jnp.zeros((16, LANES), jnp.float32)

    @pl.loop(0, 256)
    def _(i):
        acc[i] = jnp.zeros((8, LANES), jnp.float32)

    for copy in copies:
        copy.wait()

    even = lax.rem(sub, 2) == 0

    @pl.loop(0, 128)
    def _(s):
        g = s // 16
        for k in range(8):
            lane = lax.rem(s, 16) * 8 + k
            place = smem_i[g, 0, lane]
            shift = smem_i[g, 1, lane]
            target = smem_i[g, 2, lane]
            c0, s0 = smem_f[g, 3, lane], smem_f[g, 4, lane]
            c1, s1 = smem_f[g, 5, lane], smem_f[g, 6, lane]
            first = lanes >= shift
            m0 = jnp.where(first, prof[pl.ds(place, 8), :], prof[pl.ds(place + 2, 8), :])
            m1 = jnp.where(first, prof[pl.ds(place + ROWS, 8), :], prof[pl.ds(place + ROWS + 2, 8), :])
            straight = c0 * m0 + c1 * m1
            crossed = s0 * m0 + s1 * m1
            crossed = jnp.where(even, -pltpu.roll(crossed, 7, 0), pltpu.roll(crossed, 1, 0))
            acc[target] += pltpu.roll(straight + crossed, lax.rem(LANES - shift, LANES), 1)

    for o in range(4):
        part_ref[o] = acc[o * 64 : o * 64 + 64].reshape(512, LANES).astype(jnp.bfloat16)

    for i in range(8):
        fine = jnp.dot(interp_ref[...], prior_ref[i], preferred_element_type=jnp.float32)
        base_ref[pl.ds(i, 64, stride=8), :] = fine
    base_ref[...] += acc[pl.ds((1 + c) * 64, 64)].reshape(512, LANES)


def merge(prof, meta, prior, interp):
    vmem = pl.BlockSpec(memory_space=pltpu.VMEM)
    return pl.pallas_call(
        merge_kernel,
        out_shape=(
            jax.ShapeDtypeStruct((4, 512, LANES), jnp.bfloat16),
            jax.ShapeDtypeStruct((512, LANES), jnp.float32),
        ),
        in_specs=[vmem] * 4,
        out_specs=(vmem, vmem),
        scratch_shapes=[
            pltpu.VMEM((32 * ROWS + 16, LANES), jnp.float32),
            pltpu.VMEM((256, 8, LANES), jnp.float32),
            pltpu.VMEM((8, 8, LANES), jnp.int32),
            pltpu.VMEM((8, 8, LANES), jnp.float32),
            pltpu.SMEM((8, 8, LANES), jnp.int32),
            pltpu.SMEM((8, 8, LANES), jnp.float32),
            pltpu.SemaphoreType.DMA((2,)),
        ],
        compiler_params=pltpu.CompilerParams(vmem_limit_bytes=40 << 20),
        name="merge",
    )(prof, meta, prior, interp)


def exchange_kernel(part_ref, got_ref, send_sem, recv_sem):
    z, x, y, c = position()
    barrier = pltpu.get_barrier_semaphore()
    offsets = [jnp.where(c == 0, a, b) for a, b in ((-1, -2), (1, -1), (2, 1))]
    index = [jnp.where(c == 0, a, b) for a, b in ((0, 0), (2, 1), (3, 3))]
    for offset in offsets:
        pl.semaphore_signal(barrier, inc=1, device_id=at(z + offset, x, y, c), device_id_type=MESH)
        pl.semaphore_signal(barrier, inc=1, device_id=at(z - offset, x, y, c), device_id_type=MESH)
    pl.semaphore_wait(barrier, 6)
    copies = []
    for n in (2, 0, 1):
        copy = pltpu.make_async_remote_copy(
            src_ref=part_ref.at[index[n]], dst_ref=got_ref.at[n],
            send_sem=send_sem.at[n], recv_sem=recv_sem.at[n],
            device_id=at(z + offsets[n], x, y, c), device_id_type=MESH,
        )
        copy.start()
        copies.append(copy)
    for copy in copies:
        copy.wait()


def exchange(part):
    return pl.pallas_call(
        exchange_kernel,
        out_shape=jax.ShapeDtypeStruct((3, 512, LANES), jnp.bfloat16),
        in_specs=[pl.BlockSpec(memory_space=pl.ANY)],
        out_specs=pl.BlockSpec(memory_space=pl.ANY),
        scratch_shapes=[pltpu.SemaphoreType.DMA((3,)), pltpu.SemaphoreType.DMA((3,))],
        compiler_params=pltpu.CompilerParams(collective_id=1, has_side_effects=True, vmem_limit_bytes=16 << 20),
        name="exchange",
    )(part)


def on_device(
    echo, chirp_phase, rec_phase, rec_start, rec_owner, rec_row, rec_weight, rec_count, prior, interp_weight
):
    taps = chirp_phase.shape[0]
    unit = 1.0 / jnp.sqrt(jnp.float32(taps))

    def rounded(values):
        return values.astype(jnp.bfloat16).astype(jnp.float32)

    tap_cos = rounded(jnp.cos(chirp_phase) * unit)[None]
    tap_sin = rounded(jnp.sin(chirp_phase) * unit)[None]
    phases = rec_phase[0].T
    echo_rows = echo.reshape(2, 2, 32, LANES).transpose(0, 2, 1, 3).reshape(LANES, LANES)
    prof, meta = gather(
        echo_rows, tap_cos, tap_sin, rounded(jnp.cos(phases)), rounded(jnp.sin(phases)),
        rec_start, rec_owner[:, :, 0], rec_owner[0], rec_row, rec_weight, rec_count,
    )
    prior_rows = prior.reshape(32, 2, 4, LANES).transpose(2, 1, 0, 3).reshape(8, 32, LANES)
    part, base = merge(prof.reshape(2, 16, ROWS, LANES), meta.reshape(LANES, 8, LANES), prior_rows, interp_weight)
    got = exchange(part)
    total = base + got[0].astype(jnp.float32) + got[1].astype(jnp.float32) + got[2].astype(jnp.float32)
    return total.reshape(64, 4, 2, LANES).transpose(0, 2, 1, 3).reshape(64, 2, 4 * LANES)


def solution(mesh):
    placed = (
        P("pulse", None, "range"),
        P(),
        P("range", "pulse", None),
        P("range", "pulse"),
        P("range", "pulse", None),
        P("range", "pulse"),
        P("range", "pulse"),
        P("range", "pulse"),
        P("pulse", None, "range"),
        P(),
    )
    return jax.shard_map(
        on_device, mesh=mesh, in_specs=placed, out_specs=P("pulse", None, "range"), check_vma=False
    )
```

```python
import jax
import jax.numpy as jnp
from jax import lax
from jax.experimental import pallas as pl
from jax.experimental.pallas import tpu as pltpu
from jax.sharding import PartitionSpec as P

MESH = pl.DeviceIdType.MESH
LANES = 128
ROWS = 512
NT = (((1,), (1,)), ((), ()))
TN = (((0,), (0,)), ((), ()))
INPUTS = 9


def position():
    pulse, rng = lax.axis_index("pulse"), lax.axis_index("range")
    return pulse // 4, lax.rem(pulse, 4), rng // 2, lax.rem(rng, 2)


def at(z, x, y, c):
    return (lax.rem(z + 16, 16) * 4 + lax.rem(x + 4, 4), lax.rem(y + 4, 4) * 2 + c)


def swap_planes(rows):
    count = rows.shape[0]
    even = lax.rem(lax.broadcasted_iota(jnp.int32, rows.shape, 0), 2) == 0
    return jnp.where(even, pltpu.roll(rows, count - 1, 0), -pltpu.roll(rows, 1, 0))


def describe(phase, start, owner, row, weight, count):
    shape = (LANES, LANES)
    lanes = lax.broadcasted_iota(jnp.int32, (1, LANES), 1)
    number = owner[...].astype(jnp.float32)
    across = jnp.broadcast_to(number, shape)
    earlier = lax.broadcasted_iota(jnp.int32, shape, 0) < lax.broadcasted_iota(jnp.int32, shape, 1)
    same = (across.T == across) & earlier
    rank = jnp.sum(same.astype(jnp.float32), axis=0, keepdims=True)
    live = lanes < count[0, 0]
    key = jnp.where(live, number * 2.0 + rank, -1.0)
    scale = jnp.where(live, weight[...], 0.0) * jnp.float32(0.5**0.5)
    fields = [key] + [
        field.astype(jnp.float32) for field in (start[...] // LANES, lax.rem(start[...], LANES), row[...])
    ]
    for k in range(2):
        for turn in (jnp.cos, jnp.sin):
            fields.append(scale * turn(phase[k : k + 1, :]).astype(jnp.bfloat16).astype(jnp.float32))
    which = lax.broadcasted_iota(jnp.int32, (8, LANES), 0)
    tile = jnp.zeros((8, LANES), jnp.float32)
    for place, field in enumerate(fields):
        tile = jnp.where(which == place, field, tile)
    return tile


def tap_band(chirp):
    bands = []
    for turn in (jnp.cos, jnp.sin):
        taps = turn(chirp[...]) * jnp.float32(1 / 16)
        taps = jnp.concatenate([taps, jnp.zeros((1, LANES), jnp.float32)], axis=1)
        taps = jnp.broadcast_to(taps, (LANES, 3 * LANES))
        bands.append(pltpu.roll(taps, 0, 1, stride=1, stride_axis=0).astype(jnp.bfloat16))
    return jnp.concatenate(bands, axis=1)


def kernel(*refs):
    given, count, out_ref, held = refs[:INPUTS], refs[INPUTS], refs[INPUTS + 1], refs[INPUTS + 2 : 2 * INPUTS + 2]
    echo, chirp, phase, start, owner, row, weight, prior, interp = held
    (
        in_sem, ext, halo, raw, meta, prof, slots, rows, codes, sel, smem, stage, part, got, coarse, base, smem_sem,
        halo_s, halo_r, z_s, z_r, mz_s, mz_r, a_s, a_r, b_s, b_r, t_s, t_r, e_s, e_r,
    ) = refs[2 * INPUTS + 2 :]
    z, x, y, c = position()
    rng = y * 2 + c
    pulse = lax.axis_index("pulse")
    twin = at(z, x, y, 1 - c)
    before, after = (pulse, lax.rem(rng + 7, 8)), (pulse, lax.rem(rng + 1, 8))

    loads = [pltpu.make_async_copy(src, dst, in_sem.at[n]) for n, (src, dst) in enumerate(zip(given, held))]
    for load in loads:
        load.start()
    barrier = pltpu.get_barrier_semaphore()
    partners = [twin, before, after]
    for d in (1, 2, 3):
        partners += [at(z + 4 * d, x, y, c), at(z, x + d, y, c), at(z, x, y + d, c)]
    for d in (-2, -1, 1, 2):
        partners.append(at(z + d, x, y, c))
    for partner in partners:
        pl.semaphore_signal(barrier, inc=1, device_id=partner, device_id_type=MESH)
    for load in loads:
        load.wait()

    meta[0, x, y, c] = describe(phase, start, owner, row, weight, count)
    for k in range(2):
        ext[k, 0:64, :] = echo[k * 64 : k * 64 + 64, :].astype(jnp.float32)
        halo[0, k * 4 : k * 4 + 4, :] = ext[k, 0:4, :]
    band = tap_band(chirp)
    pl.semaphore_wait(barrier, len(partners))

    sends = []

    def send(src, dst, s, r, to):
        copy = pltpu.make_async_remote_copy(
            src_ref=src, dst_ref=dst, send_sem=s, recv_sem=r, device_id=to, device_id_type=MESH
        )
        copy.start()
        sends.append(copy)
        return copy

    def arrived(copies):
        for copy in copies:
            copy.wait_recv()

    halo_copy = send(halo.at[0], halo.at[1], halo_s, halo_r, before)
    mz = {
        d: send(
            meta.at[0, x, y, c], meta.at[4 - d, x, y, c], mz_s.at[d - 1], mz_r.at[d - 1], at(z + 4 * d, x, y, c)
        )
        for d in (2, 1, 3)
    }
    arrived([halo_copy])
    inside = (rng < 7).astype(jnp.float32)
    for k in range(2):
        ext[k, 64:68, :] = halo[1, k * 4 : k * 4 + 4, :] * inside
        ext[k, 68:72, :] = jnp.zeros((4, LANES), jnp.float32)
    for k in range(2):
        whole = ext[k]
        swapped = swap_planes(whole)
        parts = [whole[2 * d : 2 * d + 64] for d in range(3)] + [swapped[2 * d : 2 * d + 64] for d in range(3)]
        windows = jnp.concatenate([piece.astype(jnp.bfloat16) for piece in parts], axis=1)
        filtered = lax.dot_general(windows, band, NT, preferred_element_type=jnp.float32)
        raw[0, k, x, y, c] = filtered.astype(jnp.bfloat16)
    zs = {
        d: send(
            raw.at[0, :, x, y, c], raw.at[4 - d, :, x, y, c], z_s.at[d - 1], z_r.at[d - 1], at(z + 4 * d, x, y, c)
        )
        for d in (2, 1, 3)
    }

    def spread(n, cut, x_first):
        here = cut(x, y)
        return [
            send(
                here, here, a_s.at[n, d - 1], a_r.at[n, d - 1],
                at(z, x + d, y, c) if x_first else at(z, x, y + d, c),
            )
            for d in (1, 3, 2)
        ]

    def spread_line(n, cut, x_first):
        line = cut(slice(None), y) if x_first else cut(x, slice(None))
        again = {
            d: send(
                line, line, b_s.at[n, d - 1], b_r.at[n, d - 1],
                at(z, x, y + d, c) if x_first else at(z, x + d, y, c),
            )
            for d in (1, 3, 2)
        }
        return again, [send(line, line, t_s.at[n, 0], t_r.at[n, 0], twin)]

    def to_twin(n, cut, x_first, state):
        again, over = state
        for d, copy in again.items():
            copy.wait_recv()
            line = cut(slice(None), lax.rem(y + 4 - d, 4)) if x_first else cut(lax.rem(x + 4 - d, 4), slice(None))
            over.append(send(line, line, t_s.at[n, d], t_r.at[n, d], twin))
        return over

    def cut_of(zrel, k):
        return lambda x_, y_: raw.at[zrel, k, x_, y_, c]

    def cut_meta(x_, y_):
        return meta.at[:, x_, y_, c]

    class PlaneSet:
        def __init__(self, zrel):
            self.kinds = [(zrel * 2 + k, cut_of(zrel, k), k == 0) for k in range(2)]

        def first(self):
            self.along = [spread(*kind) for kind in self.kinds]

        def second(self):
            self.states = []
            for kind, along in zip(self.kinds, self.along):
                arrived(along)
                self.states.append(spread_line(*kind))

        def third(self):
            self.over = []
            for kind, state in zip(self.kinds, self.states):
                self.over += to_twin(*kind, state)

    planes = [PlaneSet(zrel) for zrel in range(4)]
    meta_kind = (8, cut_meta, True)

    lanes = lax.broadcasted_iota(jnp.int32, (8, LANES), 1)
    lane1 = lanes[0:1, :]
    sub = lax.broadcasted_iota(jnp.int32, (8, LANES), 0)
    even = lax.rem(sub, 2) == 0
    keys = []
    for k in range(8):
        zo = lax.rem(z + (k // 2) + 15 - c, 16)
        keys.append(((((zo * 4 + x) * 8) + rng) * 2 + k % 2).astype(jnp.float32))

    def select():
        @pl.loop(0, 8)
        def _(g):
            found = [jnp.full((1, LANES), -1.0, jnp.float32) for _ in range(4)]
            for t in range(16):
                tile = meta[g // 2, lax.rem(g, 2) * 2 + t // 8, t % 8 // 2, t % 2]
                key = tile[0:1, :]
                code = tile[1:2, :] * 16384.0 + tile[2:3, :] * 128.0
                tile = jnp.where(sub == 0, code, tile)
                line = jnp.zeros((1, LANES), jnp.float32)
                for k in range(8):
                    one = jnp.sum(jnp.where(key == keys[k], tile, 0.0), axis=1, keepdims=True)
                    one = jnp.broadcast_to(one, (8, LANES))
                    slots[(g * 16 + t) * 8 + k] = one
                    line = jnp.where(lane1 == k, one[0:1, :], line)
                    found[k // 2] = jnp.where(lane1 == t * 2 + k % 2, one[3:4, :], found[k // 2])
                codes[pl.ds(g * 16 + t, 1), :] = line
            for o in range(4):
                rows[g, o : o + 1, :] = found[o]

        sel[...] = codes[...].astype(jnp.int32)
        copy = pltpu.make_async_copy(sel, smem, smem_sem)
        copy.start()
        copy.wait()

    def form(zrel):
        arrived(planes[zrel].over)

        @pl.loop(0, 4)
        def _(p):
            base_row = (zrel * 4 + p) * (2 * ROWS)
            for k in range(2):
                at_row = pl.multiple_of(base_row + k * ROWS, ROWS)
                prof[pl.ds(at_row, ROWS), :] = raw[zrel, k, p].reshape(ROWS, LANES).astype(jnp.float32)

        @pl.loop(zrel * 4, zrel * 4 + 4)
        def _(p):
            made = []
            for k in range(64):
                s = p * 8 + k // 8
                code = smem[s, k % 8]
                place = p * (2 * ROWS) + ((code >> 13) & 510)
                turn = (code >> 7) & (LANES - 1)
                slot = slots.at[s * 8 + k % 8]
                first = lanes.astype(jnp.float32) >= slot[2:3, :]
                c0, s0, c1, s1 = (slot[i : i + 1, :] for i in range(4, 8))
                m0 = jnp.where(first, prof[pl.ds(place, 8), :], prof[pl.ds(place + 2, 8), :])
                m1 = jnp.where(first, prof[pl.ds(place + ROWS, 8), :], prof[pl.ds(place + ROWS + 2, 8), :])
                straight = c0 * m0 + c1 * m1
                crossed = s0 * m0 + s1 * m1
                crossed = jnp.where(even, -pltpu.roll(crossed, 7, 0), pltpu.roll(crossed, 1, 0))
                made.append(pltpu.roll(straight + crossed, (LANES - turn) & (LANES - 1), 1))
            for k, record in enumerate(made):
                s = p * 8 + k // 8
                stage[k % 8 // 2, pl.ds(s * 2 + k % 2, 8, stride=256), :] = record

    prof[32 * ROWS : 32 * ROWS + 16, :] = jnp.zeros((16, LANES), jnp.float32)
    planes[0].first()
    arrived(mz.values())
    along = spread(*meta_kind)
    planes[0].second()
    arrived(along)
    meta_state = spread_line(*meta_kind)
    arrived([zs[1]])
    planes[3].first()
    arrived([zs[3]])
    planes[1].first()
    over = to_twin(*meta_kind, meta_state)
    planes[0].third()
    planes[3].second()
    planes[1].second()
    arrived(over)
    select()
    arrived([zs[2]])
    planes[2].first()
    form(0)
    planes[2].second()
    planes[3].third()
    planes[1].third()
    form(3)
    planes[2].third()
    form(1)
    form(2)

    def total(o, i, marks):
        records = stage[o, i * 256 : i * 256 + 256, :].astype(jnp.bfloat16)
        return jnp.dot(marks, records, preferred_element_type=jnp.float32)

    def marks_of(o):
        row_of = jnp.concatenate([rows[g, pl.ds(o, 1), 0:32] for g in range(8)], axis=1)
        level = lax.broadcasted_iota(jnp.int32, (64, 256), 0).astype(jnp.float32)
        return (level == row_of).astype(jnp.bfloat16)

    parts_sent = []
    for n, (low, high) in enumerate(((3, 0), (0, 1), (2, 3))):
        o = jnp.where(c == 0, low, high)
        marks = marks_of(o)
        for i in range(8):
            part[n, i * 64 : i * 64 + 64, :] = total(o, i, marks).astype(jnp.bfloat16)
        parts_sent.append(send(part.at[n], got.at[n], e_s.at[n], e_r.at[n], at(z + o - 1 - c, x, y, c)))

    coarse[...] = prior[...].astype(jnp.float32)
    marks = marks_of(1 + c)
    for i in range(8):
        piece = coarse[pl.ds(i, 32, stride=8), :].astype(jnp.bfloat16)
        fine = lax.dot_general(interp[...], piece, TN, preferred_element_type=jnp.float32)
        base[i * 64 : i * 64 + 64, :] = fine + total(1 + c, i, marks)
    arrived(parts_sent)
    for i in range(8):
        whole = base[i * 64 : i * 64 + 64, :]
        for n in range(3):
            whole = whole + got[n, i * 64 : i * 64 + 64, :].astype(jnp.float32)
        out_ref[pl.ds(i, 64, stride=8), :] = whole
    for copy in sends:
        copy.wait_send()


def merged(*inputs):
    anywhere = pl.BlockSpec(memory_space=pl.ANY)
    dma = pltpu.SemaphoreType.DMA
    f32, bf16 = jnp.float32, jnp.bfloat16
    return pl.pallas_call(
        kernel,
        out_shape=jax.ShapeDtypeStruct((512, LANES), f32),
        in_specs=[anywhere] * INPUTS + [pl.BlockSpec(memory_space=pltpu.SMEM)],
        out_specs=pl.BlockSpec(memory_space=pltpu.VMEM),
        scratch_shapes=[pltpu.VMEM(a.shape, a.dtype) for a in inputs[:INPUTS]]
        + [
            dma((INPUTS,)),
            pltpu.VMEM((2, 72, LANES), f32),
            pltpu.VMEM((2, 8, LANES), f32),
            pltpu.VMEM((4, 2, 4, 4, 2, 64, LANES), bf16),
            pltpu.VMEM((4, 4, 4, 2, 8, LANES), f32),
            pltpu.VMEM((32 * ROWS + 16, LANES), f32),
            pltpu.VMEM((1024, 8, LANES), f32),
            pltpu.VMEM((8, 8, LANES), f32),
            pltpu.VMEM((LANES, LANES), f32),
            pltpu.VMEM((LANES, LANES), jnp.int32),
            pltpu.SMEM((LANES, LANES), jnp.int32),
            pltpu.VMEM((4, 2048, LANES), f32),
            pltpu.VMEM((3, 512, LANES), bf16),
            pltpu.VMEM((3, 512, LANES), bf16),
            pltpu.VMEM((256, LANES), f32),
            pltpu.VMEM((512, LANES), f32),
            dma,
            dma, dma, dma((3,)), dma((3,)), dma((3,)), dma((3,)),
            dma((9, 3)), dma((9, 3)), dma((9, 3)), dma((9, 3)), dma((9, 4)), dma((9, 4)),
            dma((3,)), dma((3,)),
        ],
        compiler_params=pltpu.CompilerParams(collective_id=0, has_side_effects=True, vmem_limit_bytes=56 << 20),
        name="merged",
    )(*inputs)


def on_device(
    echo, chirp_phase, rec_phase, rec_start, rec_owner, rec_row, rec_weight, rec_count, prior, interp_weight
):
    def by_block(array):
        count, blocks = array.shape[0], array.shape[2] // LANES
        array = array.reshape(count, 2, blocks, LANES).transpose(0, 2, 1, 3)
        return array.reshape(count * blocks * 2, LANES)

    tiles = merged(
        by_block(echo), chirp_phase[None], rec_phase[0].T, rec_start, rec_owner[:, :, 0], rec_row, rec_weight,
        by_block(prior), interp_weight.T, rec_count,
    )
    return tiles.reshape(64, 4, 2, LANES).transpose(0, 2, 1, 3).reshape(64, 2, 4 * LANES)


def solution(mesh):
    placed = (
        P("pulse", None, "range"),
        P(),
        P("range", "pulse", None),
        P("range", "pulse"),
        P("range", "pulse", None),
        P("range", "pulse"),
        P("range", "pulse"),
        P("range", "pulse"),
        P("pulse", None, "range"),
        P(),
    )
    return jax.shard_map(
        on_device, mesh=mesh, in_specs=placed, out_specs=P("pulse", None, "range"), check_vma=False
    )
```

```python
import jax
import jax.numpy as jnp
from jax import lax
from jax.experimental import pallas as pl
from jax.experimental.pallas import tpu as pltpu
from jax.sharding import PartitionSpec as P

MESH = pl.DeviceIdType.MESH
LANES = 128
ROWS = 512
NT = (((1,), (1,)), ((), ()))
TN = (((0,), (0,)), ((), ()))
INPUTS = 9


def position():
    pulse, rng = lax.axis_index("pulse"), lax.axis_index("range")
    return pulse // 4, lax.rem(pulse, 4), rng // 2, lax.rem(rng, 2)


def at(z, x, y, c):
    return (lax.rem(z + 16, 16) * 4 + lax.rem(x + 4, 4), lax.rem(y + 4, 4) * 2 + c)


def swap_planes(rows):
    count = rows.shape[0]
    even = lax.rem(lax.broadcasted_iota(jnp.int32, rows.shape, 0), 2) == 0
    return jnp.where(even, pltpu.roll(rows, count - 1, 0), -pltpu.roll(rows, 1, 0))


def describe(phase, start, owner, row, weight, count):
    shape = (LANES, LANES)
    lanes = lax.broadcasted_iota(jnp.int32, (1, LANES), 1)
    number = owner[...].astype(jnp.float32)
    across = jnp.broadcast_to(number, shape)
    earlier = lax.broadcasted_iota(jnp.int32, shape, 0) < lax.broadcasted_iota(jnp.int32, shape, 1)
    same = (across.T == across) & earlier
    rank = jnp.sum(same.astype(jnp.float32), axis=0, keepdims=True)
    live = lanes < count[0, 0]
    key = jnp.where(live, number * 2.0 + rank, -1.0)
    scale = jnp.where(live, weight[...], 0.0) * jnp.float32(0.5**0.5)
    fields = [key] + [
        field.astype(jnp.float32) for field in (start[...] // LANES, lax.rem(start[...], LANES), row[...])
    ]
    for k in range(2):
        for turn in (jnp.cos, jnp.sin):
            fields.append(scale * turn(phase[k : k + 1, :]).astype(jnp.bfloat16).astype(jnp.float32))
    which = lax.broadcasted_iota(jnp.int32, (8, LANES), 0)
    tile = jnp.zeros((8, LANES), jnp.float32)
    for place, field in enumerate(fields):
        tile = jnp.where(which == place, field, tile)
    return tile


def tap_band(chirp):
    bands = []
    for turn in (jnp.cos, jnp.sin):
        taps = turn(chirp[...]) * jnp.float32(1 / 16)
        taps = jnp.concatenate([taps, jnp.zeros((1, LANES), jnp.float32)], axis=1)
        taps = jnp.broadcast_to(taps, (LANES, 3 * LANES))
        bands.append(pltpu.roll(taps, 0, 1, stride=1, stride_axis=0).astype(jnp.bfloat16))
    return jnp.concatenate(bands, axis=1)


def kernel(*refs):
    given, count, out_ref, held = refs[:INPUTS], refs[INPUTS], refs[INPUTS + 1], refs[INPUTS + 2 : 2 * INPUTS + 2]
    echo, chirp, phase, start, owner, row, weight, prior, interp = held
    (
        in_sem, ext, halo, raw, meta, prof, slots, rows, codes, sel, smem, stage, part, got, coarse, base, smem_sem,
        halo_s, halo_r, z_s, z_r, mz_s, mz_r, a_s, a_r, b_s, b_r, t_s, t_r, e_s, e_r,
    ) = refs[2 * INPUTS + 2 :]
    z, x, y, c = position()
    rng = y * 2 + c
    pulse = lax.axis_index("pulse")
    twin = at(z, x, y, 1 - c)
    before, after = (pulse, lax.rem(rng + 7, 8)), (pulse, lax.rem(rng + 1, 8))

    loads = [pltpu.make_async_copy(src, dst, in_sem.at[n]) for n, (src, dst) in enumerate(zip(given, held))]
    for load in loads:
        load.start()
    barrier = pltpu.get_barrier_semaphore()
    partners = [twin, before, after]
    for d in (1, 2, 3):
        partners += [at(z + 4 * d, x, y, c), at(z, x + d, y, c), at(z, x, y + d, c)]
    for d in (-2, -1, 1, 2):
        partners.append(at(z + d, x, y, c))
    for partner in partners:
        pl.semaphore_signal(barrier, inc=1, device_id=partner, device_id_type=MESH)
    for load in loads:
        load.wait()

    meta[0, x, y, c] = describe(phase, start, owner, row, weight, count)
    for k in range(2):
        ext[k, 0:64, :] = echo[k * 64 : k * 64 + 64, :].astype(jnp.float32)
        halo[0, k * 4 : k * 4 + 4, :] = ext[k, 0:4, :]
    band = tap_band(chirp)
    pl.semaphore_wait(barrier, len(partners))

    sends = []

    def send(src, dst, s, r, to):
        copy = pltpu.make_async_remote_copy(
            src_ref=src, dst_ref=dst, send_sem=s, recv_sem=r, device_id=to, device_id_type=MESH
        )
        copy.start()
        sends.append(copy)
        return copy

    def arrived(copies):
        for copy in copies:
            copy.wait_recv()

    halo_copy = send(halo.at[0], halo.at[1], halo_s, halo_r, before)
    mz = {
        d: send(
            meta.at[0, x, y, c], meta.at[4 - d, x, y, c], mz_s.at[d - 1], mz_r.at[d - 1], at(z + 4 * d, x, y, c)
        )
        for d in (2, 1, 3)
    }
    arrived([halo_copy])
    inside = (rng < 7).astype(jnp.float32)
    for k in range(2):
        ext[k, 64:68, :] = halo[1, k * 4 : k * 4 + 4, :] * inside
        ext[k, 68:72, :] = jnp.zeros((4, LANES), jnp.float32)
    for k in range(2):
        whole = ext[k]
        swapped = swap_planes(whole)
        parts = [whole[2 * d : 2 * d + 64] for d in range(3)] + [swapped[2 * d : 2 * d + 64] for d in range(3)]
        windows = jnp.concatenate([piece.astype(jnp.bfloat16) for piece in parts], axis=1)
        filtered = lax.dot_general(windows, band, NT, preferred_element_type=jnp.float32)
        raw[0, k, x, y, c] = filtered.astype(jnp.bfloat16)
    zs = {
        d: send(
            raw.at[0, :, x, y, c], raw.at[4 - d, :, x, y, c], z_s.at[d - 1], z_r.at[d - 1], at(z + 4 * d, x, y, c)
        )
        for d in (2, 1, 3)
    }

    def spread(n, cut, x_first):
        here = cut(x, y)
        return [
            send(
                here, here, a_s.at[n, d - 1], a_r.at[n, d - 1],
                at(z, x + d, y, c) if x_first else at(z, x, y + d, c),
            )
            for d in (1, 3, 2)
        ]

    def spread_line(n, cut, x_first):
        line = cut(slice(None), y) if x_first else cut(x, slice(None))
        again = {
            d: send(
                line, line, b_s.at[n, d - 1], b_r.at[n, d - 1],
                at(z, x, y + d, c) if x_first else at(z, x + d, y, c),
            )
            for d in (1, 3, 2)
        }
        return again, [send(line, line, t_s.at[n, 0], t_r.at[n, 0], twin)]

    def to_twin(n, cut, x_first, state):
        again, over = state
        for d, copy in again.items():
            copy.wait_recv()
            line = cut(slice(None), lax.rem(y + 4 - d, 4)) if x_first else cut(lax.rem(x + 4 - d, 4), slice(None))
            over.append(send(line, line, t_s.at[n, d], t_r.at[n, d], twin))
        return over

    def cut_of(zrel, k):
        return lambda x_, y_: raw.at[zrel, k, x_, y_, c]

    def cut_meta(x_, y_):
        return meta.at[:, x_, y_, c]

    class PlaneSet:
        def __init__(self, zrel):
            self.kinds = [(zrel * 2 + k, cut_of(zrel, k), k == 0) for k in range(2)]

        def first(self):
            self.along = [spread(*kind) for kind in self.kinds]

        def second(self):
            self.states = []
            for kind, along in zip(self.kinds, self.along):
                arrived(along)
                self.states.append(spread_line(*kind))

        def third(self):
            self.over = []
            for kind, state in zip(self.kinds, self.states):
                self.over += to_twin(*kind, state)

    planes = [PlaneSet(zrel) for zrel in range(4)]
    meta_kind = (8, cut_meta, True)

    lanes = lax.broadcasted_iota(jnp.int32, (8, LANES), 1)
    lane1 = lanes[0:1, :]
    sub = lax.broadcasted_iota(jnp.int32, (8, LANES), 0)
    even = lax.rem(sub, 2) == 0
    keys = []
    for k in range(8):
        zo = lax.rem(z + (k // 2) + 15 - c, 16)
        keys.append(((((zo * 4 + x) * 8) + rng) * 2 + k % 2).astype(jnp.float32))

    def select():
        @pl.loop(0, 8)
        def _(g):
            found = [jnp.full((1, LANES), -1.0, jnp.float32) for _ in range(4)]
            for t in range(16):
                tile = meta[g // 2, lax.rem(g, 2) * 2 + t // 8, t % 8 // 2, t % 2]
                key = tile[0:1, :]
                code = tile[1:2, :] * 16384.0 + tile[2:3, :] * 128.0
                tile = jnp.where(sub == 0, code, tile)
                line = jnp.zeros((1, LANES), jnp.float32)
                for k in range(8):
                    one = jnp.sum(jnp.where(key == keys[k], tile, 0.0), axis=1, keepdims=True)
                    one = jnp.broadcast_to(one, (8, LANES))
                    slots[(g * 16 + t) * 8 + k] = one
                    line = jnp.where(lane1 == k, one[0:1, :], line)
                    found[k // 2] = jnp.where(lane1 == t * 2 + k % 2, one[3:4, :], found[k // 2])
                codes[pl.ds(g * 16 + t, 1), :] = line
            for o in range(4):
                rows[g, o : o + 1, :] = found[o]

        sel[...] = codes[...].astype(jnp.int32)
        copy = pltpu.make_async_copy(sel, smem, smem_sem)
        copy.start()
        copy.wait()

    def form(zrel):
        arrived(planes[zrel].over)

        @pl.loop(0, 4)
        def _(p):
            base_row = (zrel * 4 + p) * (2 * ROWS)
            for k in range(2):
                at_row = pl.multiple_of(base_row + k * ROWS, ROWS)
                prof[pl.ds(at_row, ROWS), :] = raw[zrel, k, p].reshape(ROWS, LANES).astype(jnp.float32)

        @pl.loop(zrel * 4, zrel * 4 + 4)
        def _(p):
            made = []
            for k in range(64):
                s = p * 8 + k // 8
                code = smem[s, k % 8]
                place = p * (2 * ROWS) + ((code >> 13) & 510)
                turn = (code >> 7) & (LANES - 1)
                slot = slots.at[s * 8 + k % 8]
                first = lanes.astype(jnp.float32) >= slot[2:3, :]
                c0, s0, c1, s1 = (slot[i : i + 1, :] for i in range(4, 8))
                m0 = jnp.where(first, prof[pl.ds(place, 8), :], prof[pl.ds(place + 2, 8), :])
                m1 = jnp.where(first, prof[pl.ds(place + ROWS, 8), :], prof[pl.ds(place + ROWS + 2, 8), :])
                straight = c0 * m0 + c1 * m1
                crossed = s0 * m0 + s1 * m1
                crossed = jnp.where(even, -pltpu.roll(crossed, 7, 0), pltpu.roll(crossed, 1, 0))
                made.append(pltpu.roll(straight + crossed, (LANES - turn) & (LANES - 1), 1))
            for k, record in enumerate(made):
                s = p * 8 + k // 8
                stage[k % 8 // 2, pl.ds(s * 2 + k % 2, 8, stride=256), :] = record

    prof[32 * ROWS : 32 * ROWS + 16, :] = jnp.zeros((16, LANES), jnp.float32)
    planes[0].first()
    planes[0].second()
    arrived(mz.values())
    along = spread(*meta_kind)
    for d in (1, 3, 2):
        arrived([zs[d]])
        planes[4 - d].first()
    arrived(along)
    meta_state = spread_line(*meta_kind)
    planes[0].third()
    for zrel in (3, 1, 2):
        planes[zrel].second()
    over = to_twin(*meta_kind, meta_state)
    arrived(over)
    select()
    planes[3].third()
    form(0)
    planes[1].third()
    form(3)
    planes[2].third()
    form(1)
    form(2)

    def total(o, i, marks):
        records = stage[o, i * 256 : i * 256 + 256, :].astype(jnp.bfloat16)
        return jnp.dot(marks, records, preferred_element_type=jnp.float32)

    def marks_of(o):
        row_of = jnp.concatenate([rows[g, pl.ds(o, 1), 0:32] for g in range(8)], axis=1)
        level = lax.broadcasted_iota(jnp.int32, (64, 256), 0).astype(jnp.float32)
        return (level == row_of).astype(jnp.bfloat16)

    parts_sent = []
    for n, (low, high) in enumerate(((3, 0), (0, 1), (2, 3))):
        o = jnp.where(c == 0, low, high)
        marks = marks_of(o)
        for i in range(8):
            part[n, i * 64 : i * 64 + 64, :] = total(o, i, marks).astype(jnp.bfloat16)
        parts_sent.append(send(part.at[n], got.at[n], e_s.at[n], e_r.at[n], at(z + o - 1 - c, x, y, c)))

    coarse[...] = prior[...].astype(jnp.float32)
    marks = marks_of(1 + c)
    for i in range(8):
        piece = coarse[pl.ds(i, 32, stride=8), :].astype(jnp.bfloat16)
        fine = lax.dot_general(interp[...], piece, TN, preferred_element_type=jnp.float32)
        base[i * 64 : i * 64 + 64, :] = fine + total(1 + c, i, marks)
    arrived(parts_sent)
    for i in range(8):
        whole = base[i * 64 : i * 64 + 64, :]
        for n in range(3):
            whole = whole + got[n, i * 64 : i * 64 + 64, :].astype(jnp.float32)
        out_ref[pl.ds(i, 64, stride=8), :] = whole
    for copy in sends:
        copy.wait_send()


def merged(*inputs):
    anywhere = pl.BlockSpec(memory_space=pl.ANY)
    dma = pltpu.SemaphoreType.DMA
    f32, bf16 = jnp.float32, jnp.bfloat16
    return pl.pallas_call(
        kernel,
        out_shape=jax.ShapeDtypeStruct((512, LANES), f32),
        in_specs=[anywhere] * INPUTS + [pl.BlockSpec(memory_space=pltpu.SMEM)],
        out_specs=pl.BlockSpec(memory_space=pltpu.VMEM),
        scratch_shapes=[pltpu.VMEM(a.shape, a.dtype) for a in inputs[:INPUTS]]
        + [
            dma((INPUTS,)),
            pltpu.VMEM((2, 72, LANES), f32),
            pltpu.VMEM((2, 8, LANES), f32),
            pltpu.VMEM((4, 2, 4, 4, 2, 64, LANES), bf16),
            pltpu.VMEM((4, 4, 4, 2, 8, LANES), f32),
            pltpu.VMEM((32 * ROWS + 16, LANES), f32),
            pltpu.VMEM((1024, 8, LANES), f32),
            pltpu.VMEM((8, 8, LANES), f32),
            pltpu.VMEM((LANES, LANES), f32),
            pltpu.VMEM((LANES, LANES), jnp.int32),
            pltpu.SMEM((LANES, LANES), jnp.int32),
            pltpu.VMEM((4, 2048, LANES), f32),
            pltpu.VMEM((3, 512, LANES), bf16),
            pltpu.VMEM((3, 512, LANES), bf16),
            pltpu.VMEM((256, LANES), f32),
            pltpu.VMEM((512, LANES), f32),
            dma,
            dma, dma, dma((3,)), dma((3,)), dma((3,)), dma((3,)),
            dma((9, 3)), dma((9, 3)), dma((9, 3)), dma((9, 3)), dma((9, 4)), dma((9, 4)),
            dma((3,)), dma((3,)),
        ],
        compiler_params=pltpu.CompilerParams(collective_id=0, has_side_effects=True, vmem_limit_bytes=56 << 20),
        name="merged",
    )(*inputs)


def on_device(
    echo, chirp_phase, rec_phase, rec_start, rec_owner, rec_row, rec_weight, rec_count, prior, interp_weight
):
    def by_block(array):
        count, blocks = array.shape[0], array.shape[2] // LANES
        array = array.reshape(count, 2, blocks, LANES).transpose(0, 2, 1, 3)
        return array.reshape(count * blocks * 2, LANES)

    tiles = merged(
        by_block(echo), chirp_phase[None], rec_phase[0].T, rec_start, rec_owner[:, :, 0], rec_row, rec_weight,
        by_block(prior), interp_weight.T, rec_count,
    )
    return tiles.reshape(64, 4, 2, LANES).transpose(0, 2, 1, 3).reshape(64, 2, 4 * LANES)


def solution(mesh):
    placed = (
        P("pulse", None, "range"),
        P(),
        P("range", "pulse", None),
        P("range", "pulse"),
        P("range", "pulse", None),
        P("range", "pulse"),
        P("range", "pulse"),
        P("range", "pulse"),
        P("pulse", None, "range"),
        P(),
    )
    return jax.shard_map(
        on_device, mesh=mesh, in_specs=placed, out_specs=P("pulse", None, "range"), check_vma=False
    )
```

```python
import jax
import jax.numpy as jnp
from jax import lax
from jax.experimental import pallas as pl
from jax.experimental.pallas import tpu as pltpu
from jax.sharding import PartitionSpec as P

MESH = pl.DeviceIdType.MESH
LANES = 128
ROWS = 512
NT = (((1,), (1,)), ((), ()))
TN = (((0,), (0,)), ((), ()))
INPUTS = 9


def position():
    pulse, rng = lax.axis_index("pulse"), lax.axis_index("range")
    return pulse // 4, lax.rem(pulse, 4), rng // 2, lax.rem(rng, 2)


def at(z, x, y, c):
    return (lax.rem(z + 16, 16) * 4 + lax.rem(x + 4, 4), lax.rem(y + 4, 4) * 2 + c)


def swap_planes(rows):
    count = rows.shape[0]
    even = lax.rem(lax.broadcasted_iota(jnp.int32, rows.shape, 0), 2) == 0
    return jnp.where(even, pltpu.roll(rows, count - 1, 0), -pltpu.roll(rows, 1, 0))


def describe(phase, start, owner, row, weight, count):
    shape = (LANES, LANES)
    lanes = lax.broadcasted_iota(jnp.int32, (1, LANES), 1)
    number = owner[...].astype(jnp.float32)
    across = jnp.broadcast_to(number, shape)
    earlier = lax.broadcasted_iota(jnp.int32, shape, 0) < lax.broadcasted_iota(jnp.int32, shape, 1)
    same = (across.T == across) & earlier
    rank = jnp.sum(same.astype(jnp.float32), axis=0, keepdims=True)
    live = lanes < count[0, 0]
    key = jnp.where(live, number * 2.0 + rank, -1.0)
    scale = jnp.where(live, weight[...], 0.0) * jnp.float32(0.5**0.5)
    fields = [key] + [
        field.astype(jnp.float32) for field in (start[...] // LANES, lax.rem(start[...], LANES), row[...])
    ]
    for k in range(2):
        for turn in (jnp.cos, jnp.sin):
            fields.append(scale * turn(phase[k : k + 1, :]).astype(jnp.bfloat16).astype(jnp.float32))
    which = lax.broadcasted_iota(jnp.int32, (8, LANES), 0)
    tile = jnp.zeros((8, LANES), jnp.float32)
    for place, field in enumerate(fields):
        tile = jnp.where(which == place, field, tile)
    return tile


def tap_band(chirp):
    bands = []
    for turn in (jnp.cos, jnp.sin):
        taps = turn(chirp[...]) * jnp.float32(1 / 16)
        taps = jnp.concatenate([taps, jnp.zeros((1, LANES), jnp.float32)], axis=1)
        taps = jnp.broadcast_to(taps, (LANES, 3 * LANES))
        bands.append(pltpu.roll(taps, 0, 1, stride=1, stride_axis=0).astype(jnp.bfloat16))
    return jnp.concatenate(bands, axis=1)


def kernel(*refs):
    given, count, out_ref, held = refs[:INPUTS], refs[INPUTS], refs[INPUTS + 1], refs[INPUTS + 2 : 2 * INPUTS + 2]
    echo, chirp, phase, start, owner, row, weight, prior, interp = held
    (
        in_sem, ext, halo, raw, meta, prof, slots, rows, codes, sel, smem, stage, part, got, coarse, base, smem_sem,
        halo_s, halo_r, z_s, z_r, mz_s, mz_r, a_s, a_r, b_s, b_r, t_s, t_r, e_s, e_r,
    ) = refs[2 * INPUTS + 2 :]
    z, x, y, c = position()
    rng = y * 2 + c
    pulse = lax.axis_index("pulse")
    twin = at(z, x, y, 1 - c)
    before, after = (pulse, lax.rem(rng + 7, 8)), (pulse, lax.rem(rng + 1, 8))

    loads = [pltpu.make_async_copy(src, dst, in_sem.at[n]) for n, (src, dst) in enumerate(zip(given, held))]
    for load in loads:
        load.start()
    barrier = pltpu.get_barrier_semaphore()
    partners = [twin, before, after]
    for d in (1, 2, 3):
        partners += [at(z + 4 * d, x, y, c), at(z, x + d, y, c), at(z, x, y + d, c)]
    for d in (-2, -1, 1, 2):
        partners.append(at(z + d, x, y, c))
    for partner in partners:
        pl.semaphore_signal(barrier, inc=1, device_id=partner, device_id_type=MESH)
    for load in loads:
        load.wait()

    meta[0, x, y, c] = describe(phase, start, owner, row, weight, count)
    for k in range(2):
        ext[k, 0:64, :] = echo[k * 64 : k * 64 + 64, :].astype(jnp.float32)
        halo[0, k * 4 : k * 4 + 4, :] = ext[k, 0:4, :]
    band = tap_band(chirp)
    pl.semaphore_wait(barrier, len(partners))

    sends = []

    def send(src, dst, s, r, to):
        copy = pltpu.make_async_remote_copy(
            src_ref=src, dst_ref=dst, send_sem=s, recv_sem=r, device_id=to, device_id_type=MESH
        )
        copy.start()
        sends.append(copy)
        return copy

    def arrived(copies):
        for copy in copies:
            copy.wait_recv()

    halo_copy = send(halo.at[0], halo.at[1], halo_s, halo_r, before)
    mz = {
        d: send(
            meta.at[0, x, y, c], meta.at[4 - d, x, y, c], mz_s.at[d - 1], mz_r.at[d - 1], at(z + 4 * d, x, y, c)
        )
        for d in (2, 1, 3)
    }
    arrived([halo_copy])
    inside = (rng < 7).astype(jnp.float32)
    for k in range(2):
        ext[k, 64:68, :] = halo[1, k * 4 : k * 4 + 4, :] * inside
        ext[k, 68:72, :] = jnp.zeros((4, LANES), jnp.float32)
    for k in range(2):
        whole = ext[k]
        swapped = swap_planes(whole)
        parts = [whole[2 * d : 2 * d + 64] for d in range(3)] + [swapped[2 * d : 2 * d + 64] for d in range(3)]
        windows = jnp.concatenate([piece.astype(jnp.bfloat16) for piece in parts], axis=1)
        filtered = lax.dot_general(windows, band, NT, preferred_element_type=jnp.float32)
        raw[0, k, x, y, c] = filtered.astype(jnp.bfloat16)
    zs = {
        d: send(
            raw.at[0, :, x, y, c], raw.at[4 - d, :, x, y, c], z_s.at[d - 1], z_r.at[d - 1], at(z + 4 * d, x, y, c)
        )
        for d in (2, 1, 3)
    }

    def spread(n, cut, x_first):
        here = cut(x, y)
        return [
            send(
                here, here, a_s.at[n, d - 1], a_r.at[n, d - 1],
                at(z, x + d, y, c) if x_first else at(z, x, y + d, c),
            )
            for d in (1, 3, 2)
        ]

    def spread_line(n, cut, x_first):
        line = cut(slice(None), y) if x_first else cut(x, slice(None))
        again = {
            d: send(
                line, line, b_s.at[n, d - 1], b_r.at[n, d - 1],
                at(z, x, y + d, c) if x_first else at(z, x + d, y, c),
            )
            for d in (1, 3, 2)
        }
        return again, [send(line, line, t_s.at[n, 0], t_r.at[n, 0], twin)]

    def to_twin(n, cut, x_first, state):
        again, over = state
        for d, copy in again.items():
            copy.wait_recv()
            line = cut(slice(None), lax.rem(y + 4 - d, 4)) if x_first else cut(lax.rem(x + 4 - d, 4), slice(None))
            over.append(send(line, line, t_s.at[n, d], t_r.at[n, d], twin))
        return over

    def cut_of(zrel, k):
        return lambda x_, y_: raw.at[zrel, k, x_, y_, c]

    def cut_meta(half):
        return lambda x_, y_: meta.at[pl.ds(2 * half, 2), x_, y_, c]

    class PlaneSet:
        def __init__(self, zrel):
            self.kinds = [(zrel * 2 + k, cut_of(zrel, k), k == 0) for k in range(2)]

        def first(self):
            self.along = [spread(*kind) for kind in self.kinds]

        def second(self):
            self.states = []
            for kind, along in zip(self.kinds, self.along):
                arrived(along)
                self.states.append(spread_line(*kind))

        def third(self):
            self.over = []
            for kind, state in zip(self.kinds, self.states):
                self.over += to_twin(*kind, state)

    planes = [PlaneSet(zrel) for zrel in range(4)]
    meta_kinds = [(8 + half, cut_meta(half), half == 0) for half in range(2)]

    lanes = lax.broadcasted_iota(jnp.int32, (8, LANES), 1)
    lane1 = lanes[0:1, :]
    sub = lax.broadcasted_iota(jnp.int32, (8, LANES), 0)
    even = lax.rem(sub, 2) == 0
    keys = []
    for k in range(8):
        zo = lax.rem(z + (k // 2) + 15 - c, 16)
        keys.append(((((zo * 4 + x) * 8) + rng) * 2 + k % 2).astype(jnp.float32))

    def select():
        @pl.loop(0, 8)
        def _(g):
            found = [jnp.full((1, LANES), -1.0, jnp.float32) for _ in range(4)]
            for t in range(16):
                tile = meta[g // 2, lax.rem(g, 2) * 2 + t // 8, t % 8 // 2, t % 2]
                key = tile[0:1, :]
                code = tile[1:2, :] * 16384.0 + tile[2:3, :] * 128.0
                tile = jnp.where(sub == 0, code, tile)
                line = jnp.zeros((1, LANES), jnp.float32)
                for k in range(8):
                    one = jnp.sum(jnp.where(key == keys[k], tile, 0.0), axis=1, keepdims=True)
                    one = jnp.broadcast_to(one, (8, LANES))
                    slots[(g * 16 + t) * 8 + k] = one
                    line = jnp.where(lane1 == k, one[0:1, :], line)
                    found[k // 2] = jnp.where(lane1 == t * 2 + k % 2, one[3:4, :], found[k // 2])
                codes[pl.ds(g * 16 + t, 1), :] = line
            for o in range(4):
                rows[g, o : o + 1, :] = found[o]

        sel[...] = codes[...].astype(jnp.int32)
        copy = pltpu.make_async_copy(sel, smem, smem_sem)
        copy.start()
        copy.wait()

    def form(zrel):
        arrived(planes[zrel].over)

        @pl.loop(0, 4)
        def _(p):
            base_row = (zrel * 4 + p) * (2 * ROWS)
            for k in range(2):
                at_row = pl.multiple_of(base_row + k * ROWS, ROWS)
                prof[pl.ds(at_row, ROWS), :] = raw[zrel, k, p].reshape(ROWS, LANES).astype(jnp.float32)

        @pl.loop(zrel * 4, zrel * 4 + 4)
        def _(p):
            made = []
            for k in range(64):
                s = p * 8 + k // 8
                code = smem[s, k % 8]
                place = p * (2 * ROWS) + ((code >> 13) & 510)
                turn = (code >> 7) & (LANES - 1)
                slot = slots.at[s * 8 + k % 8]
                first = lanes.astype(jnp.float32) >= slot[2:3, :]
                c0, s0, c1, s1 = (slot[i : i + 1, :] for i in range(4, 8))
                m0 = jnp.where(first, prof[pl.ds(place, 8), :], prof[pl.ds(place + 2, 8), :])
                m1 = jnp.where(first, prof[pl.ds(place + ROWS, 8), :], prof[pl.ds(place + ROWS + 2, 8), :])
                straight = c0 * m0 + c1 * m1
                crossed = s0 * m0 + s1 * m1
                crossed = jnp.where(even, -pltpu.roll(crossed, 7, 0), pltpu.roll(crossed, 1, 0))
                made.append(pltpu.roll(straight + crossed, (LANES - turn) & (LANES - 1), 1))
            for k, record in enumerate(made):
                s = p * 8 + k // 8
                stage[k % 8 // 2, pl.ds(s * 2 + k % 2, 8, stride=256), :] = record

    prof[32 * ROWS : 32 * ROWS + 16, :] = jnp.zeros((16, LANES), jnp.float32)
    planes[0].first()
    planes[0].second()
    arrived(mz.values())
    alongs = [spread(*kind) for kind in meta_kinds]
    for d in (1, 3, 2):
        arrived([zs[d]])
        planes[4 - d].first()
    meta_states = []
    for kind, along in zip(meta_kinds, alongs):
        arrived(along)
        meta_states.append(spread_line(*kind))
    planes[0].third()
    for zrel in (3, 1, 2):
        planes[zrel].second()
    overs = [to_twin(*kind, state) for kind, state in zip(meta_kinds, meta_states)]
    for over in overs:
        arrived(over)
    select()
    planes[3].third()
    form(0)
    planes[1].third()
    form(3)
    planes[2].third()
    form(1)
    form(2)

    def total(o, i, marks):
        records = stage[o, i * 256 : i * 256 + 256, :].astype(jnp.bfloat16)
        return jnp.dot(marks, records, preferred_element_type=jnp.float32)

    def marks_of(o):
        row_of = jnp.concatenate([rows[g, pl.ds(o, 1), 0:32] for g in range(8)], axis=1)
        level = lax.broadcasted_iota(jnp.int32, (64, 256), 0).astype(jnp.float32)
        return (level == row_of).astype(jnp.bfloat16)

    parts_sent = []
    for n, (low, high) in enumerate(((3, 0), (0, 1), (2, 3))):
        o = jnp.where(c == 0, low, high)
        marks = marks_of(o)
        for i in range(8):
            part[n, i * 64 : i * 64 + 64, :] = total(o, i, marks).astype(jnp.bfloat16)
        parts_sent.append(send(part.at[n], got.at[n], e_s.at[n], e_r.at[n], at(z + o - 1 - c, x, y, c)))

    coarse[...] = prior[...].astype(jnp.float32)
    marks = marks_of(1 + c)
    for i in range(8):
        piece = coarse[pl.ds(i, 32, stride=8), :].astype(jnp.bfloat16)
        fine = lax.dot_general(interp[...], piece, TN, preferred_element_type=jnp.float32)
        base[i * 64 : i * 64 + 64, :] = fine + total(1 + c, i, marks)
    arrived(parts_sent)
    for i in range(8):
        whole = base[i * 64 : i * 64 + 64, :]
        for n in range(3):
            whole = whole + got[n, i * 64 : i * 64 + 64, :].astype(jnp.float32)
        out_ref[pl.ds(i, 64, stride=8), :] = whole
    for copy in sends:
        copy.wait_send()


def merged(*inputs):
    anywhere = pl.BlockSpec(memory_space=pl.ANY)
    dma = pltpu.SemaphoreType.DMA
    f32, bf16 = jnp.float32, jnp.bfloat16
    return pl.pallas_call(
        kernel,
        out_shape=jax.ShapeDtypeStruct((512, LANES), f32),
        in_specs=[anywhere] * INPUTS + [pl.BlockSpec(memory_space=pltpu.SMEM)],
        out_specs=pl.BlockSpec(memory_space=pltpu.VMEM),
        scratch_shapes=[pltpu.VMEM(a.shape, a.dtype) for a in inputs[:INPUTS]]
        + [
            dma((INPUTS,)),
            pltpu.VMEM((2, 72, LANES), f32),
            pltpu.VMEM((2, 8, LANES), f32),
            pltpu.VMEM((4, 2, 4, 4, 2, 64, LANES), bf16),
            pltpu.VMEM((4, 4, 4, 2, 8, LANES), f32),
            pltpu.VMEM((32 * ROWS + 16, LANES), f32),
            pltpu.VMEM((1024, 8, LANES), f32),
            pltpu.VMEM((8, 8, LANES), f32),
            pltpu.VMEM((LANES, LANES), f32),
            pltpu.VMEM((LANES, LANES), jnp.int32),
            pltpu.SMEM((LANES, LANES), jnp.int32),
            pltpu.VMEM((4, 2048, LANES), f32),
            pltpu.VMEM((3, 512, LANES), bf16),
            pltpu.VMEM((3, 512, LANES), bf16),
            pltpu.VMEM((256, LANES), f32),
            pltpu.VMEM((512, LANES), f32),
            dma,
            dma, dma, dma((3,)), dma((3,)), dma((3,)), dma((3,)),
            dma((10, 3)), dma((10, 3)), dma((10, 3)), dma((10, 3)), dma((10, 4)), dma((10, 4)),
            dma((3,)), dma((3,)),
        ],
        compiler_params=pltpu.CompilerParams(collective_id=0, has_side_effects=True, vmem_limit_bytes=56 << 20),
        name="merged",
    )(*inputs)


def on_device(
    echo, chirp_phase, rec_phase, rec_start, rec_owner, rec_row, rec_weight, rec_count, prior, interp_weight
):
    def by_block(array):
        count, blocks = array.shape[0], array.shape[2] // LANES
        array = array.reshape(count, 2, blocks, LANES).transpose(0, 2, 1, 3)
        return array.reshape(count * blocks * 2, LANES)

    tiles = merged(
        by_block(echo), chirp_phase[None], rec_phase[0].T, rec_start, rec_owner[:, :, 0], rec_row, rec_weight,
        by_block(prior), interp_weight.T, rec_count,
    )
    return tiles.reshape(64, 4, 2, LANES).transpose(0, 2, 1, 3).reshape(64, 2, 4 * LANES)


def solution(mesh):
    placed = (
        P("pulse", None, "range"),
        P(),
        P("range", "pulse", None),
        P("range", "pulse"),
        P("range", "pulse", None),
        P("range", "pulse"),
        P("range", "pulse"),
        P("range", "pulse"),
        P("pulse", None, "range"),
        P(),
    )
    return jax.shard_map(
        on_device, mesh=mesh, in_specs=placed, out_specs=P("pulse", None, "range"), check_vma=False
    )
```
